32 devices in a mesh: dp: 8 (over z, y), ctx: 4 (over x, core).
Axes of the slice: x: 2, y: 2, z: 4, core: 2. Of those that a mesh axis runs over, the one named last changes fastest.
Arguments:
- hidden_in: bfloat16 [8192, 1024], P(('dp', 'ctx')), may hold values from -120 to 120
- cotangent: bfloat16 [8192, 1024], P(('dp', 'ctx')), may hold values from -6 to 6
- block_order: int32 [8, 8], P('dp'), may hold values from 0 to 7, each once within a row
- w_query: bfloat16 [2097152], P(('dp', 'ctx')), may hold values from -0.1875 to 0.1875
- key_weight: bfloat16 [1048576], P(('dp', 'ctx')), may hold values from -0.1875 to 0.1875
- value_weight: bfloat16 [1048576], P(('dp', 'ctx')), may hold values from -0.1875 to 0.1875
- w_out: bfloat16 [2097152], P(('dp', 'ctx')), may hold values from -1 to 1
- w_gate: bfloat16 [3145728], P(('dp', 'ctx')), may hold values from -0.1875 to 0.1875
- w_up: bfloat16 [3145728], P(('dp', 'ctx')), may hold values from -0.1875 to 0.1875
- w_down: bfloat16 [3145728], P(('dp', 'ctx')), may hold values from -0.109375 to 0.109375
- norm_gains: bfloat16 [2304], P(('dp', 'ctx')), may hold values from 0.099609375 to 1.8984375
Outputs:
- block_out: bfloat16 [8192, 1024], P(('dp', 'ctx'))
- grad_in: float32 [8192, 1024], P(('dp', 'ctx'))
- grad_query: float32 [2097152], P(('dp', 'ctx'))
- grad_key: float32 [1048576], P(('dp', 'ctx'))
- grad_value: float32 [1048576], P(('dp', 'ctx'))
- grad_out: float32 [2097152], P(('dp', 'ctx'))
- grad_gate: float32 [3145728], P(('dp', 'ctx'))
- grad_up: float32 [3145728], P(('dp', 'ctx'))
- grad_down: float32 [3145728], P(('dp', 'ctx'))
- grad_gains: float32 [2304], P(('dp', 'ctx'))
The draws below stay inside these ranges and needn't reach their ends.
Inputs may be any that keep to these rules, and one draw needn't show every extreme that they name: Each row is a permutation of 0 to 7; stored block j of sequence s holds positions block_order[s, j] * 128 onward.
All inputs are finite; a program needn't handle non-finite values.
Results may differ from the reference program's by a relative error of at most 0.015.
Values may be sent and summed in bfloat16 or wider, within the bound.
A program may use at most 256 MiB of HBM per device.

```python
import math
import jax
import jax.numpy as jnp
from jax import lax

MODEL_WIDTH = 1024
QUERY_HEADS = 16
KEY_VALUE_HEADS = 8
HEAD_SIZE = 128
FEEDFORWARD_UNITS = 3072
BLOCKS = 8
BLOCK = 128
SEQUENCE_TOKENS = 1024
SEQS = 8
TOKENS = 8192


def draw_hidden_in(key, part):
    key = jax.random.fold_in(key, 11)
    key_rows = jax.random.split(key, 3)
    row_scale = jnp.exp(jax.random.uniform(key_rows[0], (TOKENS, 1), minval=0.0, maxval=math.log(10.0)))
    col_scale = jnp.exp(jax.random.uniform(key_rows[1], (1, MODEL_WIDTH), minval=math.log(0.5), maxval=math.log(2.0)))
    base = jnp.clip(jax.random.normal(key_rows[2], (TOKENS, MODEL_WIDTH)), -6.0, 6.0)
    return (base * row_scale * col_scale).astype(jnp.float32).astype(jnp.bfloat16)


def shard_levels(rng, dims, cuts, least, high):
    def one(position, parts):
        steps = jax.random.uniform(jax.random.fold_in(jax.random.fold_in(rng, 6), position), (parts,), jnp.float32, least / len(cuts), high / len(cuts))
        return jnp.repeat(jnp.exp(steps), dims[position] // parts).reshape((-1,) + (1,) * (len(dims) - position - 1))

    loudness = one(*cuts[0])
    for cut in cuts[1:]:
        loudness = loudness * one(*cut)
    return loudness


def centred(stream_key, extent, scale, most, cuts=(), kind=jnp.bfloat16):
    entries = scale * jax.random.normal(stream_key, extent, jnp.float32)
    if cuts:
        entries = entries * shard_levels(stream_key, extent, cuts, -0.22, 0.18)
    return jnp.clip(entries, -most, most).astype(kind)


def setup_inputs(seed: int = 0) -> dict:
    keys = jax.random.split(jax.random.key(seed), 12)
    return {
        "hidden_in": draw_hidden_in(jax.random.fold_in(keys[11], 71), 0),
        "cotangent": centred(keys[1], (TOKENS, MODEL_WIDTH), 1.0, 6.0, ((0, 32),)),
        "block_order": jax.vmap(lambda own: jax.random.permutation(own, BLOCKS))(jax.random.split(keys[2], SEQS)).reshape((SEQS, BLOCKS)).astype(jnp.int32),
        "w_query": centred(keys[3], (MODEL_WIDTH * QUERY_HEADS * HEAD_SIZE,), MODEL_WIDTH ** -0.5, 0.1875, ((0, 32),)),
        "key_weight": centred(keys[4], (MODEL_WIDTH * KEY_VALUE_HEADS * HEAD_SIZE,), MODEL_WIDTH ** -0.5, 0.1875, ((0, 32),)),
        "value_weight": centred(keys[5], (MODEL_WIDTH * KEY_VALUE_HEADS * HEAD_SIZE,), MODEL_WIDTH ** -0.5, 0.1875, ((0, 32),)),
        "w_out": centred(keys[6], (QUERY_HEADS * HEAD_SIZE * MODEL_WIDTH,), (QUERY_HEADS * HEAD_SIZE // 64) ** -0.5, 1.0, ((0, 32),)),
        "w_gate": centred(keys[7], (MODEL_WIDTH * FEEDFORWARD_UNITS,), MODEL_WIDTH ** -0.5, 0.1875, ((0, 32),)),
        "w_up": centred(keys[8], (MODEL_WIDTH * FEEDFORWARD_UNITS,), MODEL_WIDTH ** -0.5, 0.1875, ((0, 32),)),
        "w_down": centred(keys[9], (FEEDFORWARD_UNITS * MODEL_WIDTH,), FEEDFORWARD_UNITS ** -0.5, 0.109375, ((0, 32),)),
        "norm_gains": jnp.clip(1.0 + 0.18 * jax.random.normal(keys[10], (2 * MODEL_WIDTH + 2 * HEAD_SIZE,), jnp.float32), 0.099609375, 1.8984375).astype(jnp.bfloat16),
    }


NORM_EPS = 1e-06
ROPE_THETA = 1000000.0

@jax.custom_vjp
def lower_precision(v):
    return lax.optimization_barrier(v.astype(jnp.bfloat16)).astype(jnp.float32)

@jax.custom_vjp
def lower_precision_backward(v):
    return v

def low_keep(v):
    return (lower_precision(v), None)

def low_pass(kept, grad):
    return (grad,)

def back_keep(v):
    return (v, None)

def back_low(kept, grad):
    return (lower_precision(grad),)
lower_precision.defvjp(low_keep, low_pass)
lower_precision_backward.defvjp(back_keep, back_low)

def product_exact(left, right):
    return jnp.dot(left, right, precision=lax.Precision.HIGHEST)

def rotary_tables(positions):
    half_dim = HEAD_SIZE // 2
    inverse = ROPE_THETA ** (-(jnp.arange(half_dim, dtype=jnp.float32) * 2.0 / HEAD_SIZE))
    angles = positions.astype(jnp.float32)[:, None] * inverse[None, :]
    return (jnp.cos(angles)[:, None, :], jnp.sin(angles)[:, None, :])

def apply_rotary(value_rows, cosine_table, sine_table):
    half_dim = value_rows.shape[-1] // 2
    first_half = value_rows[..., :half_dim]
    second_half = value_rows[..., half_dim:]
    return jnp.concatenate([first_half * cosine_table - second_half * sine_table, second_half * cosine_table + first_half * sine_table], axis=-1)

def root_mean_normed(value_rows, gain):
    return value_rows * lax.rsqrt(lax.optimization_barrier(jnp.mean(value_rows * value_rows, axis=-1, keepdims=True)) + NORM_EPS) * gain

def layer_sequence(tokens, places, weight_tuple):
    w_query, key_weight, value_weight, w_out, w_gate, w_up, w_down, layer_gains = weight_tuple
    query_groups = QUERY_HEADS // KEY_VALUE_HEADS
    gain_one = layer_gains[:MODEL_WIDTH]
    gain_two = layer_gains[MODEL_WIDTH:2 * MODEL_WIDTH]
    query_norm_gain = layer_gains[2 * MODEL_WIDTH:2 * MODEL_WIDTH + HEAD_SIZE]
    gain_key = layer_gains[2 * MODEL_WIDTH + HEAD_SIZE:]
    cosine_table, sine_table = rotary_tables(places)
    first_normed = lower_precision(root_mean_normed(tokens, gain_one))
    query_rows = lower_precision_backward(product_exact(first_normed, w_query)).reshape(SEQUENCE_TOKENS, QUERY_HEADS, HEAD_SIZE)
    key_rows = lower_precision_backward(product_exact(first_normed, key_weight)).reshape(SEQUENCE_TOKENS, KEY_VALUE_HEADS, HEAD_SIZE)
    value_rows = lower_precision_backward(lower_precision(product_exact(first_normed, value_weight))).reshape(SEQUENCE_TOKENS, KEY_VALUE_HEADS, HEAD_SIZE)
    query_rows = lower_precision(apply_rotary(root_mean_normed(query_rows, query_norm_gain), cosine_table, sine_table)).reshape(SEQUENCE_TOKENS, KEY_VALUE_HEADS, query_groups, HEAD_SIZE)
    key_rows = lower_precision(apply_rotary(root_mean_normed(key_rows, gain_key), cosine_table, sine_table))
    raw_scores = lower_precision_backward(jnp.einsum('tkgd,nkd->kgtn', query_rows, key_rows, precision=lax.Precision.HIGHEST))
    visible = places[None, :] <= places[:, None]
    scores = jnp.where(visible, raw_scores * HEAD_SIZE ** (-0.5), -1e+30)
    probs = lower_precision(jax.nn.softmax(scores, axis=-1))
    mixed = jnp.einsum('kgtn,nkd->tkgd', probs, value_rows, precision=lax.Precision.HIGHEST).reshape(SEQUENCE_TOKENS, QUERY_HEADS * HEAD_SIZE)
    mixed = lower_precision_backward(lower_precision(mixed))
    middle = tokens + lower_precision_backward(product_exact(mixed, w_out))
    normed_two = lower_precision(root_mean_normed(middle, gain_two))
    gate_act = lower_precision_backward(product_exact(normed_two, w_gate))
    up_act = lower_precision_backward(product_exact(normed_two, w_up))
    hidden_act = lower_precision(jax.nn.silu(gate_act) * up_act)
    return middle + lower_precision_backward(product_exact(hidden_act, w_down))

def reference(hidden_in, cotangent, block_order, w_query, key_weight, value_weight, w_out, w_gate, w_up, w_down, norm_gains):
    places = (block_order[:, :, None] * BLOCK + jnp.arange(BLOCK, dtype=jnp.int32)[None, None, :]).reshape(SEQS, SEQUENCE_TOKENS)
    floats = (hidden_in.astype(jnp.float32), w_query.astype(jnp.float32), key_weight.astype(jnp.float32), value_weight.astype(jnp.float32), w_out.astype(jnp.float32), w_gate.astype(jnp.float32), w_up.astype(jnp.float32), w_down.astype(jnp.float32), norm_gains.astype(jnp.float32))

    def forward(inputs, query_weight_flat, key_weight_flat, value_weight_flat, output_weight_flat, gate_weight_flat, up_weight_flat, down_weight_flat, layer_gains):
        weight_tuple = (query_weight_flat.reshape(MODEL_WIDTH, QUERY_HEADS * HEAD_SIZE), key_weight_flat.reshape(MODEL_WIDTH, KEY_VALUE_HEADS * HEAD_SIZE), value_weight_flat.reshape(MODEL_WIDTH, KEY_VALUE_HEADS * HEAD_SIZE), output_weight_flat.reshape(QUERY_HEADS * HEAD_SIZE, MODEL_WIDTH), gate_weight_flat.reshape(MODEL_WIDTH, FEEDFORWARD_UNITS), up_weight_flat.reshape(MODEL_WIDTH, FEEDFORWARD_UNITS), down_weight_flat.reshape(FEEDFORWARD_UNITS, MODEL_WIDTH), layer_gains)

        def one_sequence(paired):
            return layer_sequence(paired[0], paired[1], weight_tuple)
        outputs = lax.map(jax.checkpoint(one_sequence), (inputs.reshape(SEQS, SEQUENCE_TOKENS, MODEL_WIDTH), places))
        return outputs.reshape(TOKENS, MODEL_WIDTH)
    result, pullback = jax.vjp(forward, *floats)
    grads = pullback(cotangent.astype(jnp.float32))
    return (result.astype(jnp.bfloat16), grads[0], grads[1], grads[2], grads[3], grads[4], grads[5], grads[6], grads[7], grads[8])
```

```python
import functools

import jax
import jax.numpy as jnp
from jax import lax
from jax.experimental import pallas as pl
from jax.experimental.pallas import tpu as pltpu
from jax.sharding import PartitionSpec as P

QUERY_HEADS = 16
KEY_VALUE_HEADS = 8
HEAD_SIZE = 128
FEEDFORWARD_UNITS = 3072
GROUPS = QUERY_HEADS // KEY_VALUE_HEADS
GROUP_WIDTH = (GROUPS + 2) * HEAD_SIZE

NORM_EPS = 1e-06
ROPE_THETA = 1000000.0
SCALE = HEAD_SIZE ** (-0.5)
BOTH = ("dp", "ctx")
bf16 = jnp.bfloat16
f32 = jnp.float32


def inv_rms(u):
    return lax.rsqrt(jnp.mean(u * u, axis=-1, keepdims=True) + NORM_EPS)


def norm_backward(u, r, gain, upstream):
    weighted = upstream * gain
    return r * weighted - u * r**3 * jnp.mean(weighted * u, axis=-1, keepdims=True)


def dot_nn(a, b):
    return lax.dot_general(a, b, (((1,), (0,)), ((), ())), preferred_element_type=f32)


def dot_tn(a, b):
    return lax.dot_general(a, b, (((0,), (0,)), ((), ())), preferred_element_type=f32)


def dot_nt(a, b):
    return lax.dot_general(a, b, (((1,), (1,)), ((), ())), preferred_element_type=f32)


def swap_halves(z):
    return pltpu.roll(z, HEAD_SIZE // 2, 1)


def rotate(z, cos, sin):
    return z * cos + swap_halves(z) * sin


def unrotate(g, cos, sin):
    return g * cos - swap_halves(g) * sin


def prepare(slot_ref, raw_ref, cos_ref, sin_ref, gains_ref, q_s, k_s, v_s):
    blocks = slot_ref.shape[0]
    size = raw_ref.shape[0] // blocks
    gain_q = gains_ref[0:1, :]
    gain_k = gains_ref[1:2, :]
    for b in range(blocks):
        src = pl.ds(pl.multiple_of(slot_ref[b] * size, size), size)
        dst = pl.ds(b * size, size)
        cos = cos_ref[src, :]
        sin = sin_ref[src, :]
        for g in range(GROUPS):
            z = raw_ref[src, g * HEAD_SIZE : (g + 1) * HEAD_SIZE]
            q_s[g, dst, :] = rotate(z * inv_rms(z) * gain_q, cos, sin).astype(bf16)
        z = raw_ref[src, GROUPS * HEAD_SIZE : (GROUPS + 1) * HEAD_SIZE]
        k_s[dst, :] = rotate(z * inv_rms(z) * gain_k, cos, sin).astype(bf16)
        v_s[dst, :] = raw_ref[src, (GROUPS + 1) * HEAD_SIZE :].astype(bf16)


def softmax_tile(q, k, start):
    scores = dot_nt(q, k) * SCALE
    rows = lax.broadcasted_iota(jnp.int32, scores.shape, 0) + start
    cols = lax.broadcasted_iota(jnp.int32, scores.shape, 1)
    scores = jnp.where(cols <= rows, scores, -1e30)
    expo = jnp.exp(scores - jnp.max(scores, axis=-1, keepdims=True))
    return expo / jnp.sum(expo, axis=-1, keepdims=True)


def forward_kernel(tile, slot_ref, raw_ref, cos_ref, sin_ref, gains_ref, o_ref, q_s, k_s, v_s, o_s):
    prepare(slot_ref, raw_ref, cos_ref, sin_ref, gains_ref, q_s, k_s, v_s)
    length = raw_ref.shape[0]
    for i in range(length // tile):
        end = (i + 1) * tile
        for g in range(GROUPS):
            p = softmax_tile(q_s[g, i * tile : end, :], k_s[:end, :], i * tile)
            o_s[i * tile : end, g * HEAD_SIZE : (g + 1) * HEAD_SIZE] = dot_nn(
                p.astype(bf16), v_s[:end, :]
            ).astype(bf16)
    blocks = slot_ref.shape[0]
    size = length // blocks
    for b in range(blocks):
        o_ref[pl.ds(pl.multiple_of(slot_ref[b] * size, size), size), :] = o_s[
            b * size : (b + 1) * size, :
        ]


def backward_kernel(
    tile, slot_ref, raw_ref, cos_ref, sin_ref, gains_ref, do_ref, d_ref, dg_ref,
    q_s, k_s, v_s, do_s, dq_s, dk_s, dv_s,
):
    prepare(slot_ref, raw_ref, cos_ref, sin_ref, gains_ref, q_s, k_s, v_s)
    length = raw_ref.shape[0]
    blocks = slot_ref.shape[0]
    size = length // blocks
    for b in range(blocks):
        do_s[b * size : (b + 1) * size, :] = do_ref[
            pl.ds(pl.multiple_of(slot_ref[b] * size, size), size), :
        ]
    dk_s[...] = jnp.zeros_like(dk_s)
    dv_s[...] = jnp.zeros_like(dv_s)
    for i in range(length // tile):
        end = (i + 1) * tile
        for g in range(GROUPS):
            q = q_s[g, i * tile : end, :]
            do = do_s[i * tile : end, g * HEAD_SIZE : (g + 1) * HEAD_SIZE]
            p = softmax_tile(q, k_s[:end, :], i * tile)
            dp = dot_nt(do, v_s[:end, :])
            delta = jnp.sum(p * dp, axis=-1, keepdims=True)
            ds = (p * (dp - delta) * SCALE).astype(bf16)
            dq_s[g, i * tile : end, :] = dot_nn(ds, k_s[:end, :])
            dk_s[:end, :] += dot_tn(ds, q)
            dv_s[:end, :] += dot_tn(p.astype(bf16), do)
    gain_q = gains_ref[0:1, :]
    gain_k = gains_ref[1:2, :]
    dgq = jnp.zeros((1, HEAD_SIZE), f32)
    dgk = jnp.zeros((1, HEAD_SIZE), f32)
    for b in range(blocks):
        src = pl.ds(pl.multiple_of(slot_ref[b] * size, size), size)
        dst = pl.ds(b * size, size)
        cos = cos_ref[src, :]
        sin = sin_ref[src, :]
        for g in range(GROUPS):
            cols = slice(g * HEAD_SIZE, (g + 1) * HEAD_SIZE)
            z = raw_ref[src, cols]
            r = inv_rms(z)
            grad = unrotate(dq_s[g, dst, :], cos, sin)
            dgq += jnp.sum(grad * z * r, axis=0, keepdims=True)
            d_ref[src, cols] = norm_backward(z, r, gain_q, grad).astype(bf16)
        cols = slice(GROUPS * HEAD_SIZE, (GROUPS + 1) * HEAD_SIZE)
        z = raw_ref[src, cols]
        r = inv_rms(z)
        grad = unrotate(dk_s[dst, :], cos, sin)
        dgk += jnp.sum(grad * z * r, axis=0, keepdims=True)
        d_ref[src, cols] = norm_backward(z, r, gain_k, grad).astype(bf16)
        d_ref[src, (GROUPS + 1) * HEAD_SIZE :] = dv_s[dst, :].astype(bf16)
    dg_ref[...] = jnp.concatenate([dgq, dgk, jnp.zeros((6, HEAD_SIZE), f32)], axis=0)[None]


def attention_specs(length):
    group = pl.BlockSpec((length, GROUP_WIDTH), lambda h, s: (0, h))
    heads = pl.BlockSpec((length, GROUPS * HEAD_SIZE), lambda h, s: (0, h))
    table = pl.BlockSpec((length, HEAD_SIZE), lambda h, s: (0, 0))
    gains = pl.BlockSpec((8, HEAD_SIZE), lambda h, s: (0, 0))
    return group, heads, table, gains


def attention_forward(slots, raw, cos, sin, gains):
    length = raw.shape[0]
    count = raw.shape[1] // GROUP_WIDTH
    group, heads, table, gain_spec = attention_specs(length)
    return pl.pallas_call(
        functools.partial(forward_kernel, 256),
        grid_spec=pltpu.PrefetchScalarGridSpec(
            num_scalar_prefetch=1,
            grid=(count,),
            in_specs=[group, table, table, gain_spec],
            out_specs=heads,
            scratch_shapes=[
                pltpu.VMEM((GROUPS, length, HEAD_SIZE), bf16),
                pltpu.VMEM((length, HEAD_SIZE), bf16),
                pltpu.VMEM((length, HEAD_SIZE), bf16),
                pltpu.VMEM((length, GROUPS * HEAD_SIZE), bf16),
            ],
        ),
        out_shape=jax.ShapeDtypeStruct((length, count * GROUPS * HEAD_SIZE), bf16),
        compiler_params=pltpu.CompilerParams(vmem_limit_bytes=40 * 2**20),
        cost_estimate=pl.CostEstimate(
            flops=count * GROUPS * 4 * length * length * HEAD_SIZE,
            bytes_accessed=length * count * GROUP_WIDTH * 4,
            transcendentals=count * GROUPS * length * length,
        ),
    )(slots, raw, cos, sin, gains)


def attention_backward(slots, raw, cos, sin, gains, grad_o):
    length = raw.shape[0]
    count = raw.shape[1] // GROUP_WIDTH
    group, heads, table, gain_spec = attention_specs(length)
    return pl.pallas_call(
        functools.partial(backward_kernel, 256),
        grid_spec=pltpu.PrefetchScalarGridSpec(
            num_scalar_prefetch=1,
            grid=(count,),
            in_specs=[group, table, table, gain_spec, heads],
            out_specs=[group, pl.BlockSpec((1, 8, HEAD_SIZE), lambda h, s: (h, 0, 0))],
            scratch_shapes=[
                pltpu.VMEM((GROUPS, length, HEAD_SIZE), bf16),
                pltpu.VMEM((length, HEAD_SIZE), bf16),
                pltpu.VMEM((length, HEAD_SIZE), bf16),
                pltpu.VMEM((length, GROUPS * HEAD_SIZE), bf16),
                pltpu.VMEM((GROUPS, length, HEAD_SIZE), f32),
                pltpu.VMEM((length, HEAD_SIZE), f32),
                pltpu.VMEM((length, HEAD_SIZE), f32),
            ],
        ),
        out_shape=[
            jax.ShapeDtypeStruct((length, count * GROUP_WIDTH), bf16),
            jax.ShapeDtypeStruct((count, 8, HEAD_SIZE), f32),
        ],
        compiler_params=pltpu.CompilerParams(vmem_limit_bytes=40 * 2**20),
        cost_estimate=pl.CostEstimate(
            flops=count * GROUPS * 10 * length * length * HEAD_SIZE,
            bytes_accessed=length * count * GROUP_WIDTH * 6,
            transcendentals=count * GROUPS * length * length,
        ),
    )(slots, raw, cos, sin, gains, grad_o)


def gather_rows(x, axis):
    return lax.all_gather(x, axis, axis=0, tiled=True)


def sum_rows(x, axis):
    return lax.psum_scatter(x.astype(bf16), axis, scatter_dimension=0, tiled=True)


def shards(
    hidden_in,
    cotangent,
    block_order,
    w_query,
    key_weight,
    value_weight,
    w_out,
    w_gate,
    w_up,
    w_down,
    norm_gains,
):
    width = hidden_in.shape[1]
    dp, ctx = lax.axis_size("dp"), lax.axis_size("ctx")
    devices = dp * ctx
    length = hidden_in.shape[0] * ctx
    units = FEEDFORWARD_UNITS // ctx
    kv_local = KEY_VALUE_HEADS // ctx
    qkv_width = kv_local * GROUP_WIDTH
    heads_width = kv_local * GROUPS * HEAD_SIZE

    orders = block_order[0]
    blocks = orders.shape[0]
    size = length // blocks
    slots = jnp.sum(
        jnp.where(
            orders[None, :] == jnp.arange(blocks, dtype=jnp.int32)[:, None],
            jnp.arange(blocks, dtype=jnp.int32)[None, :],
            0,
        ),
        axis=1,
    ).astype(jnp.int32)
    places = (orders[:, None] * size + jnp.arange(size, dtype=jnp.int32)[None, :]).reshape(-1)
    half = HEAD_SIZE // 2
    inverse = ROPE_THETA ** (-(jnp.arange(half, dtype=f32) * 2.0 / HEAD_SIZE))
    angles = places.astype(f32)[:, None] * inverse[None, :]
    cos, sin = jnp.cos(angles), jnp.sin(angles)
    cos_table = jnp.concatenate([cos, cos], axis=1)
    sin_table = jnp.concatenate([-sin, sin], axis=1)

    x_all = gather_rows(hidden_in, "ctx")
    gain_piece = norm_gains.shape[0]
    gains_all = gather_rows(
        jnp.pad(norm_gains[None, :], ((0, 15), (0, 128 - gain_piece))), BOTH
    )
    gains = gains_all.reshape(devices, 16, 128)[:, 0, :gain_piece].reshape(-1).astype(f32)
    gain_one = gains[:width]
    gain_two = gains[width : 2 * width]
    head_gains = jnp.pad(gains[2 * width :].reshape(2, HEAD_SIZE), ((0, 6), (0, 0)))

    rows = w_query.shape[0] // (QUERY_HEADS * HEAD_SIZE)
    qkv_rows = jnp.concatenate(
        [
            w_query.reshape(rows, KEY_VALUE_HEADS, GROUPS * HEAD_SIZE),
            key_weight.reshape(rows, KEY_VALUE_HEADS, HEAD_SIZE),
            value_weight.reshape(rows, KEY_VALUE_HEADS, HEAD_SIZE),
        ],
        axis=2,
    ).reshape(rows, ctx, qkv_width)
    mlp_rows = jnp.concatenate(
        [w_gate.reshape(rows, ctx, units), w_up.reshape(rows, ctx, units)], axis=2
    )
    column_rows = jnp.concatenate([qkv_rows, mlp_rows], axis=2).transpose(1, 0, 2)
    column_rows = lax.all_to_all(column_rows, "ctx", 0, 0, tiled=True)
    column_rows = column_rows.reshape(ctx * rows, -1)
    row_parts = jnp.concatenate([w_out.reshape(-1, width), w_down.reshape(-1, width)], axis=0)
    out_rows = w_out.shape[0] // width
    there = [(d, (d % dp) * ctx + d // dp) for d in range(devices)]
    back = [(b, a) for a, b in there]
    row_parts = lax.ppermute(row_parts, BOTH, there)

    qkv_w = gather_rows(column_rows[:, :qkv_width], "dp")
    out_w = gather_rows(row_parts[:out_rows], "dp")
    mlp_w = gather_rows(column_rows[:, qkv_width:], "dp")
    down_w = gather_rows(row_parts[out_rows:], "dp")
    dy_all = gather_rows(cotangent, "ctx")

    x_full = x_all.astype(f32)
    a_all = (x_full * inv_rms(x_full) * gain_one).astype(bf16)
    raw = dot_nn(a_all, qkv_w)
    o_all = attention_forward(slots, raw, cos_table, sin_table, head_gains)
    x = hidden_in.astype(f32)
    scale_one = inv_rms(x)
    middle = x + sum_rows(dot_nn(o_all, out_w), "ctx").astype(f32)
    scale_two = inv_rms(middle)
    b_all = gather_rows((middle * scale_two * gain_two).astype(bf16), "ctx")

    both = dot_nn(b_all, mlp_w)
    gate, up = both[:, :units], both[:, units:]
    sigmoid = jax.nn.sigmoid(gate)
    activated = gate * sigmoid
    hidden = (activated * up).astype(bf16)
    grad_hidden = dot_nt(dy_all, down_w)
    grad_both = jnp.concatenate(
        [
            (grad_hidden * up * sigmoid * (1.0 + gate * (1.0 - sigmoid))).astype(bf16),
            (grad_hidden * activated).astype(bf16),
        ],
        axis=1,
    )
    grad_b = sum_rows(dot_nt(grad_both, mlp_w), "ctx").astype(f32)
    block_out = (middle + sum_rows(dot_nn(hidden, down_w), "ctx").astype(f32)).astype(bf16)
    grad_mlp = sum_rows(dot_tn(b_all, grad_both), "dp")
    grad_down = sum_rows(dot_tn(hidden, dy_all), "dp")

    grad_gain_two = jnp.sum(grad_b * middle * scale_two, axis=0)
    grad_middle = cotangent.astype(f32) + norm_backward(middle, scale_two, gain_two, grad_b)
    dom_all = gather_rows(grad_middle.astype(bf16), "ctx")
    grad_o = dot_nt(dom_all, out_w).astype(bf16)
    grad_out = sum_rows(dot_tn(o_all, dom_all), "dp")
    grad_raw, grad_head_gains = attention_backward(
        slots, raw, cos_table, sin_table, head_gains, grad_o
    )
    grad_a = sum_rows(dot_nt(grad_raw, qkv_w), "ctx").astype(f32)
    grad_qkv = sum_rows(dot_tn(a_all, grad_raw), "dp")
    grad_gain_one = jnp.sum(grad_a * x * scale_one, axis=0)
    grad_in = grad_middle + norm_backward(x, scale_one, gain_one, grad_a)

    grad_gains = jnp.concatenate(
        [grad_gain_one, grad_gain_two, jnp.sum(grad_head_gains, axis=0)[:2].reshape(-1)]
    ).reshape(devices, 1, gain_piece)
    grad_gains = jnp.pad(grad_gains, ((0, 0), (0, 7), (0, 128 - gain_piece)))
    grad_gains = lax.psum_scatter(
        grad_gains.reshape(devices * 8, 128), BOTH, scatter_dimension=0, tiled=True
    )[0, :gain_piece]

    columns = jnp.concatenate([grad_qkv, grad_mlp], axis=1).reshape(ctx, rows, -1)
    columns = lax.all_to_all(columns, "ctx", 0, 0, tiled=True).transpose(1, 0, 2).astype(f32)
    own_qkv = columns[:, :, :qkv_width].reshape(rows, KEY_VALUE_HEADS, GROUP_WIDTH)
    own_mlp = columns[:, :, qkv_width:]
    row_grads = lax.ppermute(jnp.concatenate([grad_out, grad_down], axis=0), BOTH, back)
    row_grads = row_grads.astype(f32)
    split = GROUPS * HEAD_SIZE
    return (
        block_out,
        grad_in,
        own_qkv[:, :, :split].reshape(-1),
        own_qkv[:, :, split : split + HEAD_SIZE].reshape(-1),
        own_qkv[:, :, split + HEAD_SIZE :].reshape(-1),
        row_grads[:out_rows].reshape(-1),
        own_mlp[:, :, :units].reshape(-1),
        own_mlp[:, :, units:].reshape(-1),
        row_grads[out_rows:].reshape(-1),
        grad_gains,
    )


def solution(mesh):
    rows = P(("dp", "ctx"), None)
    flat = P(("dp", "ctx"))
    return jax.shard_map(
        shards,
        mesh=mesh,
        in_specs=(rows, rows, P("dp", None)) + (flat,) * 8,
        out_specs=(rows, rows) + (flat,) * 8,
        check_vma=False,
    )
```

```python
import functools

import jax
import jax.numpy as jnp
from jax import lax
from jax.experimental import pallas as pl
from jax.experimental.pallas import tpu as pltpu
from jax.sharding import PartitionSpec as P

QUERY_HEADS = 16
KEY_VALUE_HEADS = 8
HEAD_SIZE = 128
FEEDFORWARD_UNITS = 3072
GROUPS = QUERY_HEADS // KEY_VALUE_HEADS
GROUP_WIDTH = (GROUPS + 2) * HEAD_SIZE

NORM_EPS = 1e-06
ROPE_THETA = 1000000.0
SCALE = HEAD_SIZE ** (-0.5)
BOTH = ("dp", "ctx")
bf16 = jnp.bfloat16
f32 = jnp.float32


def inv_rms(u):
    return lax.rsqrt(jnp.mean(u * u, axis=-1, keepdims=True) + NORM_EPS)


def norm_backward(u, r, gain, upstream):
    weighted = upstream * gain
    return r * weighted - u * r**3 * jnp.mean(weighted * u, axis=-1, keepdims=True)


def dot_nn(a, b):
    return lax.dot_general(a, b, (((1,), (0,)), ((), ())), preferred_element_type=f32)


def dot_tn(a, b):
    return lax.dot_general(a, b, (((0,), (0,)), ((), ())), preferred_element_type=f32)


def dot_nt(a, b):
    return lax.dot_general(a, b, (((1,), (1,)), ((), ())), preferred_element_type=f32)


def swap_halves(z):
    return pltpu.roll(z, HEAD_SIZE // 2, 1)


def rotate(z, cos, sin):
    return z * cos + swap_halves(z) * sin


def unrotate(g, cos, sin):
    return g * cos - swap_halves(g) * sin


def prepare(slot_ref, raw_ref, cos_ref, sin_ref, gains_ref, q_s, k_s, v_s):
    blocks = slot_ref.shape[0]
    size = raw_ref.shape[0] // blocks
    gain_q = gains_ref[0:1, :]
    gain_k = gains_ref[1:2, :]
    for b in range(blocks):
        src = pl.ds(pl.multiple_of(slot_ref[b] * size, size), size)
        dst = pl.ds(b * size, size)
        cos = cos_ref[src, :]
        sin = sin_ref[src, :]
        for g in range(GROUPS):
            z = raw_ref[src, g * HEAD_SIZE : (g + 1) * HEAD_SIZE]
            q_s[g, dst, :] = rotate(z * inv_rms(z) * gain_q, cos, sin).astype(bf16)
        z = raw_ref[src, GROUPS * HEAD_SIZE : (GROUPS + 1) * HEAD_SIZE]
        k_s[dst, :] = rotate(z * inv_rms(z) * gain_k, cos, sin).astype(bf16)
        v_s[dst, :] = raw_ref[src, (GROUPS + 1) * HEAD_SIZE :].astype(bf16)


def softmax_tile(q, k, start):
    scores = dot_nt(q, k) * SCALE
    rows = lax.broadcasted_iota(jnp.int32, scores.shape, 0) + start
    cols = lax.broadcasted_iota(jnp.int32, scores.shape, 1)
    scores = jnp.where(cols <= rows, scores, -1e30)
    expo = jnp.exp(scores - jnp.max(scores, axis=-1, keepdims=True))
    return expo / jnp.sum(expo, axis=-1, keepdims=True)


def forward_kernel(tile, slot_ref, raw_ref, cos_ref, sin_ref, gains_ref, o_ref, q_s, k_s, v_s, o_s):
    prepare(slot_ref, raw_ref, cos_ref, sin_ref, gains_ref, q_s, k_s, v_s)
    length = raw_ref.shape[0]
    for i in range(length // tile):
        end = (i + 1) * tile
        for g in range(GROUPS):
            p = softmax_tile(q_s[g, i * tile : end, :], k_s[:end, :], i * tile)
            o_s[i * tile : end, g * HEAD_SIZE : (g + 1) * HEAD_SIZE] = dot_nn(
                p.astype(bf16), v_s[:end, :]
            ).astype(bf16)
    blocks = slot_ref.shape[0]
    size = length // blocks
    for b in range(blocks):
        o_ref[pl.ds(pl.multiple_of(slot_ref[b] * size, size), size), :] = o_s[
            b * size : (b + 1) * size, :
        ]


def backward_kernel(
    tile, slot_ref, raw_ref, cos_ref, sin_ref, gains_ref, do_ref, d_ref, dg_ref,
    q_s, k_s, v_s, do_s, dq_s, dk_s, dv_s,
):
    prepare(slot_ref, raw_ref, cos_ref, sin_ref, gains_ref, q_s, k_s, v_s)
    length = raw_ref.shape[0]
    blocks = slot_ref.shape[0]
    size = length // blocks
    for b in range(blocks):
        do_s[b * size : (b + 1) * size, :] = do_ref[
            pl.ds(pl.multiple_of(slot_ref[b] * size, size), size), :
        ]
    dk_s[...] = jnp.zeros_like(dk_s)
    dv_s[...] = jnp.zeros_like(dv_s)
    for i in range(length // tile):
        end = (i + 1) * tile
        for g in range(GROUPS):
            q = q_s[g, i * tile : end, :]
            do = do_s[i * tile : end, g * HEAD_SIZE : (g + 1) * HEAD_SIZE]
            p = softmax_tile(q, k_s[:end, :], i * tile)
            dp = dot_nt(do, v_s[:end, :])
            delta = jnp.sum(p * dp, axis=-1, keepdims=True)
            ds = (p * (dp - delta) * SCALE).astype(bf16)
            dq_s[g, i * tile : end, :] = dot_nn(ds, k_s[:end, :])
            dk_s[:end, :] += dot_tn(ds, q)
            dv_s[:end, :] += dot_tn(p.astype(bf16), do)
    gain_q = gains_ref[0:1, :]
    gain_k = gains_ref[1:2, :]
    dgq = jnp.zeros((1, HEAD_SIZE), f32)
    dgk = jnp.zeros((1, HEAD_SIZE), f32)
    for b in range(blocks):
        src = pl.ds(pl.multiple_of(slot_ref[b] * size, size), size)
        dst = pl.ds(b * size, size)
        cos = cos_ref[src, :]
        sin = sin_ref[src, :]
        for g in range(GROUPS):
            cols = slice(g * HEAD_SIZE, (g + 1) * HEAD_SIZE)
            z = raw_ref[src, cols]
            r = inv_rms(z)
            grad = unrotate(dq_s[g, dst, :], cos, sin)
            dgq += jnp.sum(grad * z * r, axis=0, keepdims=True)
            d_ref[src, cols] = norm_backward(z, r, gain_q, grad).astype(bf16)
        cols = slice(GROUPS * HEAD_SIZE, (GROUPS + 1) * HEAD_SIZE)
        z = raw_ref[src, cols]
        r = inv_rms(z)
        grad = unrotate(dk_s[dst, :], cos, sin)
        dgk += jnp.sum(grad * z * r, axis=0, keepdims=True)
        d_ref[src, cols] = norm_backward(z, r, gain_k, grad).astype(bf16)
        d_ref[src, (GROUPS + 1) * HEAD_SIZE :] = dv_s[dst, :].astype(bf16)
    dg_ref[...] = jnp.concatenate([dgq, dgk, jnp.zeros((6, HEAD_SIZE), f32)], axis=0)[None]


def attention_specs(length):
    group = pl.BlockSpec((length, GROUP_WIDTH), lambda h, s: (0, h))
    heads = pl.BlockSpec((length, GROUPS * HEAD_SIZE), lambda h, s: (0, h))
    table = pl.BlockSpec((length, HEAD_SIZE), lambda h, s: (0, 0))
    gains = pl.BlockSpec((8, HEAD_SIZE), lambda h, s: (0, 0))
    return group, heads, table, gains


def attention_forward(slots, raw, cos, sin, gains):
    length = raw.shape[0]
    count = raw.shape[1] // GROUP_WIDTH
    group, heads, table, gain_spec = attention_specs(length)
    return pl.pallas_call(
        functools.partial(forward_kernel, 256),
        grid_spec=pltpu.PrefetchScalarGridSpec(
            num_scalar_prefetch=1,
            grid=(count,),
            in_specs=[group, table, table, gain_spec],
            out_specs=heads,
            scratch_shapes=[
                pltpu.VMEM((GROUPS, length, HEAD_SIZE), bf16),
                pltpu.VMEM((length, HEAD_SIZE), bf16),
                pltpu.VMEM((length, HEAD_SIZE), bf16),
                pltpu.VMEM((length, GROUPS * HEAD_SIZE), bf16),
            ],
        ),
        out_shape=jax.ShapeDtypeStruct((length, count * GROUPS * HEAD_SIZE), bf16),
        compiler_params=pltpu.CompilerParams(vmem_limit_bytes=40 * 2**20),
        cost_estimate=pl.CostEstimate(
            flops=count * GROUPS * 4 * length * length * HEAD_SIZE,
            bytes_accessed=length * count * GROUP_WIDTH * 4,
            transcendentals=count * GROUPS * length * length,
        ),
    )(slots, raw, cos, sin, gains)


def attention_backward(slots, raw, cos, sin, gains, grad_o):
    length = raw.shape[0]
    count = raw.shape[1] // GROUP_WIDTH
    group, heads, table, gain_spec = attention_specs(length)
    return pl.pallas_call(
        functools.partial(backward_kernel, 256),
        grid_spec=pltpu.PrefetchScalarGridSpec(
            num_scalar_prefetch=1,
            grid=(count,),
            in_specs=[group, table, table, gain_spec, heads],
            out_specs=[group, pl.BlockSpec((1, 8, HEAD_SIZE), lambda h, s: (h, 0, 0))],
            scratch_shapes=[
                pltpu.VMEM((GROUPS, length, HEAD_SIZE), bf16),
                pltpu.VMEM((length, HEAD_SIZE), bf16),
                pltpu.VMEM((length, HEAD_SIZE), bf16),
                pltpu.VMEM((length, GROUPS * HEAD_SIZE), bf16),
                pltpu.VMEM((GROUPS, length, HEAD_SIZE), f32),
                pltpu.VMEM((length, HEAD_SIZE), f32),
                pltpu.VMEM((length, HEAD_SIZE), f32),
            ],
        ),
        out_shape=[
            jax.ShapeDtypeStruct((length, count * GROUP_WIDTH), bf16),
            jax.ShapeDtypeStruct((count, 8, HEAD_SIZE), f32),
        ],
        compiler_params=pltpu.CompilerParams(vmem_limit_bytes=40 * 2**20),
        cost_estimate=pl.CostEstimate(
            flops=count * GROUPS * 10 * length * length * HEAD_SIZE,
            bytes_accessed=length * count * GROUP_WIDTH * 6,
            transcendentals=count * GROUPS * length * length,
        ),
    )(slots, raw, cos, sin, gains, grad_o)


def gather_rows(x, axis):
    return lax.all_gather(x, axis, axis=0, tiled=True)


def sum_rows(x, axis):
    return lax.psum_scatter(x.astype(bf16), axis, scatter_dimension=0, tiled=True)


def shards(
    hidden_in,
    cotangent,
    block_order,
    w_query,
    key_weight,
    value_weight,
    w_out,
    w_gate,
    w_up,
    w_down,
    norm_gains,
):
    width = hidden_in.shape[1]
    dp, ctx = lax.axis_size("dp"), lax.axis_size("ctx")
    devices = dp * ctx
    length = hidden_in.shape[0] * ctx
    units = FEEDFORWARD_UNITS // ctx
    kv_local = KEY_VALUE_HEADS // ctx
    qkv_width = kv_local * GROUP_WIDTH
    heads_width = kv_local * GROUPS * HEAD_SIZE

    orders = block_order[0]
    blocks = orders.shape[0]
    size = length // blocks
    slots = jnp.sum(
        jnp.where(
            orders[None, :] == jnp.arange(blocks, dtype=jnp.int32)[:, None],
            jnp.arange(blocks, dtype=jnp.int32)[None, :],
            0,
        ),
        axis=1,
    ).astype(jnp.int32)
    places = (orders[:, None] * size + jnp.arange(size, dtype=jnp.int32)[None, :]).reshape(-1)
    half = HEAD_SIZE // 2
    inverse = ROPE_THETA ** (-(jnp.arange(half, dtype=f32) * 2.0 / HEAD_SIZE))
    angles = places.astype(f32)[:, None] * inverse[None, :]
    cos, sin = jnp.cos(angles), jnp.sin(angles)
    cos_table = jnp.concatenate([cos, cos], axis=1)
    sin_table = jnp.concatenate([-sin, sin], axis=1)

    both_all = gather_rows(jnp.concatenate([hidden_in, cotangent], axis=1), "ctx")
    x_all, dy_all = both_all[:, :width], both_all[:, width:]
    gain_piece = norm_gains.shape[0]
    gains_all = gather_rows(
        jnp.pad(norm_gains[None, :], ((0, 15), (0, 128 - gain_piece))), BOTH
    )
    gains = gains_all.reshape(devices, 16, 128)[:, 0, :gain_piece].reshape(-1).astype(f32)
    gain_one = gains[:width]
    gain_two = gains[width : 2 * width]
    head_gains = jnp.pad(gains[2 * width :].reshape(2, HEAD_SIZE), ((0, 6), (0, 0)))

    rows = w_query.shape[0] // (QUERY_HEADS * HEAD_SIZE)
    qkv_rows = jnp.concatenate(
        [
            w_query.reshape(rows, KEY_VALUE_HEADS, GROUPS * HEAD_SIZE),
            key_weight.reshape(rows, KEY_VALUE_HEADS, HEAD_SIZE),
            value_weight.reshape(rows, KEY_VALUE_HEADS, HEAD_SIZE),
        ],
        axis=2,
    ).reshape(rows, ctx, qkv_width)
    mlp_rows = jnp.concatenate(
        [w_gate.reshape(rows, ctx, units), w_up.reshape(rows, ctx, units)], axis=2
    )
    column_rows = jnp.concatenate([qkv_rows, mlp_rows], axis=2).transpose(1, 0, 2)
    column_rows = lax.all_to_all(column_rows, "ctx", 0, 0, tiled=True)
    column_rows = column_rows.reshape(ctx * rows, -1)
    row_parts = jnp.concatenate([w_out.reshape(-1, width), w_down.reshape(-1, width)], axis=0)
    out_rows = w_out.shape[0] // width
    there = [(d, (d % dp) * ctx + d // dp) for d in range(devices)]
    back = [(b, a) for a, b in there]
    row_parts = lax.ppermute(row_parts, BOTH, there)

    column_w = gather_rows(column_rows, "dp")
    qkv_w, mlp_w = column_w[:, :qkv_width], column_w[:, qkv_width:]
    row_w = gather_rows(row_parts, "dp").reshape(dp, -1, width)
    out_w = row_w[:, :out_rows].reshape(-1, width)
    down_w = row_w[:, out_rows:].reshape(-1, width)

    x_full = x_all.astype(f32)
    a_all = (x_full * inv_rms(x_full) * gain_one).astype(bf16)
    raw = dot_nn(a_all, qkv_w)
    o_all = attention_forward(slots, raw, cos_table, sin_table, head_gains)
    x = hidden_in.astype(f32)
    scale_one = inv_rms(x)
    middle = x + sum_rows(dot_nn(o_all, out_w), "ctx").astype(f32)
    scale_two = inv_rms(middle)
    b_all = gather_rows((middle * scale_two * gain_two).astype(bf16), "ctx")

    both = dot_nn(b_all, mlp_w)
    gate, up = both[:, :units], both[:, units:]
    sigmoid = jax.nn.sigmoid(gate)
    activated = gate * sigmoid
    hidden = (activated * up).astype(bf16)
    grad_hidden = dot_nt(dy_all, down_w)
    grad_both = jnp.concatenate(
        [
            (grad_hidden * up * sigmoid * (1.0 + gate * (1.0 - sigmoid))).astype(bf16),
            (grad_hidden * activated).astype(bf16),
        ],
        axis=1,
    )
    sums = sum_rows(
        jnp.concatenate(
            [dot_nt(grad_both, mlp_w).astype(bf16), dot_nn(hidden, down_w).astype(bf16)], axis=1
        ),
        "ctx",
    ).astype(f32)
    grad_b = sums[:, :width]
    block_out = (middle + sums[:, width:]).astype(bf16)
    grad_mlp = dot_tn(b_all, grad_both).astype(bf16)
    grad_down = dot_tn(hidden, dy_all).astype(bf16)

    grad_gain_two = jnp.sum(grad_b * middle * scale_two, axis=0)
    grad_middle = cotangent.astype(f32) + norm_backward(middle, scale_two, gain_two, grad_b)
    dom_all = gather_rows(grad_middle.astype(bf16), "ctx")
    grad_o = dot_nt(dom_all, out_w).astype(bf16)
    grad_out = dot_tn(o_all, dom_all).astype(bf16)
    row_grads = jnp.concatenate(
        [grad_out.reshape(dp, -1, width), grad_down.reshape(dp, -1, width)], axis=1
    )
    row_grads = sum_rows(row_grads.reshape(-1, width), "dp")
    grad_raw, grad_head_gains = attention_backward(
        slots, raw, cos_table, sin_table, head_gains, grad_o
    )
    grad_a = sum_rows(dot_nt(grad_raw, qkv_w), "ctx").astype(f32)
    grad_qkv = dot_tn(a_all, grad_raw).astype(bf16)
    grad_gain_one = jnp.sum(grad_a * x * scale_one, axis=0)
    grad_in = grad_middle + norm_backward(x, scale_one, gain_one, grad_a)

    grad_gains = jnp.concatenate(
        [grad_gain_one, grad_gain_two, jnp.sum(grad_head_gains, axis=0)[:2].reshape(-1)]
    )
    lines = grad_gains.shape[0] // 128
    grad_gains = jnp.pad(grad_gains.reshape(lines, 128), ((0, -lines % 8), (0, 0)))
    grad_gains = gather_rows(grad_gains, BOTH).reshape(devices, -1, 128)[:, :lines]
    grad_gains = lax.dynamic_slice_in_dim(
        jnp.sum(grad_gains, axis=0).reshape(-1), lax.axis_index(BOTH) * gain_piece, gain_piece
    )

    columns = sum_rows(jnp.concatenate([grad_qkv, grad_mlp], axis=1), "dp")
    columns = columns.reshape(ctx, rows, -1)
    columns = lax.all_to_all(columns, "ctx", 0, 0, tiled=True).transpose(1, 0, 2).astype(f32)
    own_qkv = columns[:, :, :qkv_width].reshape(rows, KEY_VALUE_HEADS, GROUP_WIDTH)
    own_mlp = columns[:, :, qkv_width:]
    row_grads = lax.ppermute(row_grads, BOTH, back)
    row_grads = row_grads.astype(f32)
    split = GROUPS * HEAD_SIZE
    return (
        block_out,
        grad_in,
        own_qkv[:, :, :split].reshape(-1),
        own_qkv[:, :, split : split + HEAD_SIZE].reshape(-1),
        own_qkv[:, :, split + HEAD_SIZE :].reshape(-1),
        row_grads[:out_rows].reshape(-1),
        own_mlp[:, :, :units].reshape(-1),
        own_mlp[:, :, units:].reshape(-1),
        row_grads[out_rows:].reshape(-1),
        grad_gains,
    )


def solution(mesh):
    rows = P(("dp", "ctx"), None)
    flat = P(("dp", "ctx"))
    return jax.shard_map(
        shards,
        mesh=mesh,
        in_specs=(rows, rows, P("dp", None)) + (flat,) * 8,
        out_specs=(rows, rows) + (flat,) * 8,
        check_vma=False,
    )
```
